32 devices in a mesh: field: 2 (over x), focus: 2 (over core), strip: 8 (over z, y).
Axes of the slice: x: 2, y: 2, z: 4, core: 2. Of those that a mesh axis runs over, the one named last changes fastest.
Arguments:
- slices: bfloat16 [32, 4096, 4096], P(('field', 'focus'), 'strip'), parts along dimension 0, may hold values from 0 to 1
- otf_rows: float32 [4096], replicated, may hold values from 0.1 to 1
- otf_cols: float32 [4096], replicated, may hold values from 0.1 to 1
Outputs:
- restored: float32 [8192, 4096], P(('field', 'focus', 'strip')), parts along dimension 0
The draws below stay inside these ranges and needn't reach their ends.
There are 2 independent parts, one for each index of `field`. The reference program is written for one: setup_inputs(seed, part) draws one part's arguments, and reference() takes and returns one part's arrays. A program takes and returns all parts, laid end to end along the dimension named above; an argument that names none is the same for every part. Nothing has to cross between parts.
All inputs are finite; a program needn't handle non-finite values.
Results may differ from the reference program's by a relative error of at most 0.011.
Values may be sent and summed in bfloat16 or wider, within the bound.
A program may use at most 256 MiB of HBM per device.

```python
import math
import jax
import jax.numpy as jnp
from jax import lax

N = 4096
SLICES = 16


def steps_of(key, extent, pieces, least, largest):
    level, own = 1.0, jax.random.fold_in(key, 6)
    for axis_at, blocks in pieces:
        draws = jnp.exp(jax.random.uniform(jax.random.fold_in(own, axis_at), (blocks,), jnp.float32, least / len(pieces), largest / len(pieces)))
        level = level * jnp.repeat(draws, extent[axis_at] // blocks).reshape([-1 if axis == axis_at else 1 for axis in range(len(extent))])
    return level


def setup_inputs(seed: int = 0, part: int = 0) -> dict:
    key_list = jax.random.split(jax.random.key(seed), 4)
    part_keys = jax.random.split(jax.random.fold_in(key_list[3], part), 4)
    return {
        "slices": jnp.clip(1.0 * jax.random.uniform(part_keys[0], (SLICES, N, N), jnp.float32) ** steps_of(part_keys[0], (SLICES, N, N), ((0, 2), (1, 8)), -0.2, 0.2), 0.0, 1.0).astype(jnp.bfloat16),
        "otf_rows": jnp.clip(jnp.exp(jax.random.uniform(key_list[1], (N,), jnp.float32, math.log(0.1), math.log(1.0))), 0.1, 1.0),
        "otf_cols": jnp.clip(jnp.exp(jax.random.uniform(key_list[2], (N,), jnp.float32, math.log(0.1), math.log(1.0))), 0.1, 1.0),
    }


floor_weight = 0.01
noise_ratio = 0.01

def cosine_block(first_row, height, length):
    low_count = min(64, length)
    high_count = length // low_count
    frequency = first_row + lax.broadcasted_iota(jnp.int32, (height, 1), 0)
    high_sample = lax.broadcasted_iota(jnp.int32, (1, high_count), 1)
    low_sample = lax.broadcasted_iota(jnp.int32, (1, low_count), 1)
    high_phase = 2 * low_count * high_sample * frequency % (4 * length)
    low_phase = (2 * low_sample + 1) * frequency % (4 * length)
    unit = jnp.float32(math.pi / (2 * length))
    high_angle = high_phase.astype(jnp.float32) * unit
    low_angle = low_phase.astype(jnp.float32) * unit
    norming = jnp.where(frequency == 0, jnp.float32(math.sqrt(1.0 / length)), jnp.float32(math.sqrt(2.0 / length)))
    high_cos = (norming * jnp.cos(high_angle))[:, :, None]
    high_sin = (norming * jnp.sin(high_angle))[:, :, None]
    low_cos = jnp.cos(low_angle)[:, None, :]
    low_sin = jnp.sin(low_angle)[:, None, :]
    table = high_cos * low_cos - high_sin * low_sin
    return table.reshape(height, length).astype(jnp.bfloat16)

def cosine_table(length):
    height = min(512, length)
    starts = jnp.arange(length // height, dtype=jnp.int32) * height
    return lax.map(lambda first_row: cosine_block(first_row, height, length), starts).reshape(length, length)

def laplace(picture, spacing):
    padded = jnp.pad(picture, spacing)
    total = padded[2 * spacing:, spacing:-spacing] + padded[:-2 * spacing, spacing:-spacing]
    total = total + padded[spacing:-spacing, 2 * spacing:] + padded[spacing:-spacing, :-2 * spacing]
    return total - 4.0 * picture

def matmul(left, right):
    return jnp.dot(left.astype(jnp.float32), right.astype(jnp.float32), precision=lax.Precision.HIGHEST)

def reference(slices, otf_rows, otf_cols):

    def add_slice(totals, slice_plane):
        numerator, denominator = totals
        picture = slice_plane.astype(jnp.float32)
        fine_term = laplace(picture, 1)
        middle_term = laplace(picture, 2)
        coarse_term = laplace(picture, 4)
        weight = floor_weight + fine_term * fine_term + 0.5 * middle_term * middle_term + 0.25 * coarse_term * coarse_term
        return ((numerator + weight * picture, denominator + weight), None)
    blank_field = jnp.zeros((N, N), jnp.float32)
    (numerator, denominator), _ = lax.scan(add_slice, (blank_field, blank_field), slices)
    merged_field = (numerator / denominator).astype(jnp.bfloat16)
    cosines = cosine_table(N)
    along_cols = matmul(merged_field, cosines.T).astype(jnp.bfloat16)
    spectrum = matmul(cosines, along_cols)
    response = otf_rows[:, None] * otf_cols[None, :]
    filtered = (spectrum * (response / (response * response + noise_ratio))).astype(jnp.bfloat16)
    back_cols = matmul(cosines.T, filtered).astype(jnp.bfloat16)
    return matmul(back_cols, cosines)
```

```python
import functools
import math

import jax
import jax.numpy as jnp
import numpy as np
from jax import lax
from jax.experimental import pallas as pl
from jax.experimental.pallas import tpu as pltpu
from jax.sharding import PartitionSpec as P

floor_weight = 0.01
noise_ratio = 0.01
spacings = (1, 2, 4)
margin = 4
edge = 16
lanes = 128
vmem_limit = 56 * 1024 * 1024


def band_matrices(height):
    band = np.zeros((3, height, height), np.float32)
    ends = np.zeros((3, 2, 8, 2 * edge), np.float32)
    for which, d in enumerate(spacings):
        band[which] = np.eye(height, k=d) + np.eye(height, k=-d) - 4.0 * np.eye(height)
        for r in range(d):
            ends[which, 0, r, edge + r - d] = 1.0
            ends[which, 1, 7 - r, edge + d - 1 - r] = 1.0
    return (
        jnp.asarray(band.reshape(3 * height, height), jnp.bfloat16),
        jnp.asarray(ends.reshape(48, 2 * edge), jnp.bfloat16),
    )


def cosine_table(length):
    low_count = 1 << (int(math.log2(length)) // 2)
    high_count = length // low_count
    sample = 2 * np.arange(length, dtype=np.int64) + 1
    unit = math.pi / (2 * length)
    high = (low_count * np.arange(high_count)[:, None] * sample) % (4 * length) * unit
    low = (np.arange(low_count)[:, None] * sample) % (4 * length) * unit
    scale = math.sqrt(2.0 / length)
    high_cos = jnp.asarray(scale * np.cos(high), jnp.float32)[:, None, :]
    high_sin = jnp.asarray(scale * np.sin(high), jnp.float32)[:, None, :]
    low_cos = jnp.asarray(np.cos(low), jnp.float32)[None]
    low_sin = jnp.asarray(np.sin(low), jnp.float32)[None]
    first = np.ones((high_count, low_count, 1), np.float32)
    first[0, 0] = math.sqrt(0.5)
    table = (high_cos * low_cos - high_sin * low_sin) * jnp.asarray(first)
    return table.astype(jnp.bfloat16).reshape(length, length)


def cosine_block(first_row, height, length):
    low_count = min(64, length)
    high_count = length // low_count
    frequency = first_row + lax.broadcasted_iota(jnp.int32, (height, 1), 0)
    high_sample = lax.broadcasted_iota(jnp.int32, (1, high_count), 1)
    low_sample = lax.broadcasted_iota(jnp.int32, (1, low_count), 1)
    high_phase = 2 * low_count * high_sample * frequency % (4 * length)
    low_phase = (2 * low_sample + 1) * frequency % (4 * length)
    unit = jnp.float32(math.pi / (2 * length))
    high_angle = high_phase.astype(jnp.float32) * unit
    low_angle = low_phase.astype(jnp.float32) * unit
    norming = jnp.where(
        frequency == 0, jnp.float32(math.sqrt(1.0 / length)), jnp.float32(math.sqrt(2.0 / length))
    )
    high_cos = (norming * jnp.cos(high_angle))[:, :, None]
    high_sin = (norming * jnp.sin(high_angle))[:, :, None]
    low_cos = jnp.cos(low_angle)[:, None, :]
    low_sin = jnp.sin(low_angle)[:, None, :]
    table = high_cos * low_cos - high_sin * low_sin
    return table.reshape(height, length).astype(jnp.bfloat16)


def cosine_table_plain(length):
    height = min(512, length)
    starts = jnp.arange(length // height, dtype=jnp.int32) * height
    return lax.map(lambda first_row: cosine_block(first_row, height, length), starts).reshape(
        length, length
    )


def stencil_kernel(width, half, main, top, bottom, band, ends, num, den, terms_a, terms_b):
    del half
    height, length = main.shape[1], main.shape[2]
    chunks = length // width

    @pl.when(pl.program_id(0) == 0)
    def _():
        num[...] = jnp.zeros_like(num)
        den[...] = jnp.zeros_like(den)

    def vertical(chunk, terms):
        at = pl.ds(pl.multiple_of(chunk * width, width), width)
        terms[...] = jnp.dot(band[...], main[0, :, at], preferred_element_type=jnp.float32)
        outside = jnp.concatenate([top[0, :, at], bottom[0, :, at]], axis=0)
        extra = jnp.dot(ends[...], outside, preferred_element_type=jnp.float32)
        for which in range(3):
            base = which * height
            terms[base : base + 8, :] += extra[16 * which : 16 * which + 8]
            terms[base + height - 8 : base + height, :] += extra[16 * which + 8 : 16 * which + 16]

    def weigh(chunk, terms):
        start = chunk * width
        at = pl.ds(pl.multiple_of(start, width), width)
        before = pl.ds(pl.multiple_of(jnp.maximum(start - lanes, 0), lanes), lanes)
        after = pl.ds(pl.multiple_of(jnp.minimum(start + width, length - lanes), lanes), lanes)
        has_before = jnp.where(chunk > 0, 1.0, 0.0)
        has_after = jnp.where(chunk < chunks - 1, 1.0, 0.0)
        for row in range(0, height, 16):
            rows = slice(row, row + 16)
            center = main[0, rows, at].astype(jnp.float32)
            wide = jnp.concatenate(
                [
                    main[0, rows, before].astype(jnp.float32) * has_before,
                    center,
                    main[0, rows, after].astype(jnp.float32) * has_after,
                ],
                axis=1,
            )
            full = wide.shape[1]
            lap = []
            for which, d in enumerate(spacings):
                sides = pltpu.roll(wide, d, 1) + pltpu.roll(wide, full - d, 1)
                base = which * height + row
                lap.append(terms[base : base + 16, :] + sides[:, lanes : lanes + width])
            weight = (floor_weight + lap[0] * lap[0]) + 0.5 * (
                lap[1] * lap[1] + 0.5 * (lap[2] * lap[2])
            )
            num[rows, at] += weight * center
            den[rows, at] += weight

    vertical(0, terms_a)

    def pair(index, carry):
        chunk = 2 * index
        vertical(chunk + 1, terms_b)
        weigh(chunk, terms_a)
        vertical(jnp.minimum(chunk + 2, chunks - 1), terms_a)
        weigh(chunk + 1, terms_b)
        return carry

    lax.fori_loop(0, chunks // 2, pair, 0)


def stencil(slices, half, top, bottom, height):
    count, _, length = slices.shape
    width = 256
    band, ends = band_matrices(height)
    sums = jax.ShapeDtypeStruct((height, length), jnp.float32)
    whole = lambda s, h: (0, 0)
    return pl.pallas_call(
        functools.partial(stencil_kernel, width),
        grid_spec=pltpu.PrefetchScalarGridSpec(
            num_scalar_prefetch=1,
            grid=(count,),
            in_specs=[
                pl.BlockSpec((1, height, length), lambda s, h: (s, h[0], 0)),
                pl.BlockSpec((1, edge, length), lambda s, h: (s, 0, 0)),
                pl.BlockSpec((1, edge, length), lambda s, h: (s, 0, 0)),
                pl.BlockSpec(band.shape, whole),
                pl.BlockSpec(ends.shape, whole),
            ],
            out_specs=[pl.BlockSpec((height, length), whole)] * 2,
            scratch_shapes=[pltpu.VMEM((3 * height, width), jnp.float32)] * 2,
        ),
        out_shape=(sums, sums),
        compiler_params=pltpu.CompilerParams(vmem_limit_bytes=vmem_limit),
        cost_estimate=pl.CostEstimate(
            flops=count * height * length * 1600,
            bytes_accessed=count * height * length * 2 + height * length * 8,
            transcendentals=0,
        ),
        name="stencil",
    )(half.reshape(1), slices, top, bottom, band, ends)


def product_cost(rows, length, passes):
    return pl.CostEstimate(
        flops=2 * passes * rows * length * length,
        bytes_accessed=2 * length * length + 8 * rows * length,
        transcendentals=0,
    )


def row_kernel(table, rows, out):
    value = lax.dot_general(
        table[...], rows[...], (((1,), (1,)), ((), ())), preferred_element_type=jnp.float32
    )
    out[...] = value.astype(out.dtype).reshape(out.shape)


def row_transform(cosines, rows, block):
    piece, length = rows.shape
    return pl.pallas_call(
        row_kernel,
        grid=(length // block,),
        in_specs=[
            pl.BlockSpec((block, length), lambda k: (k, 0)),
            pl.BlockSpec((piece, length), lambda k: (0, 0)),
        ],
        out_specs=pl.BlockSpec((block // piece, piece, piece), lambda k: (k, 0, 0)),
        out_shape=jax.ShapeDtypeStruct((length // piece, piece, piece), jnp.bfloat16),
        compiler_params=pltpu.CompilerParams(vmem_limit_bytes=vmem_limit),
        cost_estimate=product_cost(piece, length, 1),
        name="row_transform",
    )(cosines, rows)


def column_kernel(places, table, arrived, rows_otf, cols_otf, out, columns, total):
    piece = arrived.shape[1]
    length = table.shape[1]
    step = pl.program_id(0)

    @pl.when(step == 0)
    def _():
        for source, place in enumerate(places):
            columns[:, place * piece : (place + 1) * piece] = arrived[source]

    spectrum = lax.dot_general(
        table[...], columns[...], (((1,), (1,)), ((), ())), preferred_element_type=jnp.float32
    )
    response = rows_otf[...] * cols_otf[...]
    filtered = spectrum * (response / (response * response + noise_ratio))
    turned = filtered.T.astype(jnp.bfloat16)
    part = 512
    for start in range(0, length, part):
        at = slice(start, start + part)
        value = jnp.dot(turned, table[:, at], preferred_element_type=jnp.float32)

        @pl.when(step == 0)
        def _():
            total[:, at] = value

        @pl.when(step > 0)
        def _():
            total[:, at] += value

    @pl.when(step == pl.num_programs(0) - 1)
    def _():
        for place in range(length // piece):
            out[place] = total[:, place * piece : (place + 1) * piece].astype(out.dtype)


def column_transform(cosines, arrived, rows_otf, cols_otf, places, block):
    count, piece, _ = arrived.shape
    length = count * piece
    whole = lambda u: (0, 0, 0)
    return pl.pallas_call(
        functools.partial(column_kernel, places),
        grid=(length // block,),
        in_specs=[
            pl.BlockSpec((block, length), lambda u: (u, 0)),
            pl.BlockSpec(arrived.shape, whole),
            pl.BlockSpec((block, 1), lambda u: (u, 0)),
            pl.BlockSpec((1, piece), lambda u: (0, 0)),
        ],
        out_specs=pl.BlockSpec((count, piece, piece), whole),
        out_shape=jax.ShapeDtypeStruct((count, piece, piece), jnp.bfloat16),
        scratch_shapes=[
            pltpu.VMEM((piece, length), jnp.bfloat16),
            pltpu.VMEM((piece, length), jnp.float32),
        ],
        compiler_params=pltpu.CompilerParams(vmem_limit_bytes=vmem_limit),
        cost_estimate=product_cost(piece, length, 2),
        name="column_transform",
    )(cosines, arrived, rows_otf[:, None], cols_otf[None, :])


def final_kernel(table, back, out, rows):
    @pl.when(pl.program_id(0) == 0)
    def _():
        count, piece, _ = back.shape
        for source in range(count):
            turned = back[source].astype(jnp.float32).T
            rows[:, source * piece : (source + 1) * piece] = turned.astype(jnp.bfloat16)

    out[...] = jnp.dot(rows[...], table[...], preferred_element_type=jnp.float32)


def final_transform(cosines, back, block):
    count, piece, _ = back.shape
    length = count * piece
    return pl.pallas_call(
        final_kernel,
        grid=(length // block,),
        in_specs=[
            pl.BlockSpec((length, block), lambda n: (0, n)),
            pl.BlockSpec(back.shape, lambda n: (0, 0, 0)),
        ],
        out_specs=pl.BlockSpec((piece, block), lambda n: (0, n)),
        out_shape=jax.ShapeDtypeStruct((piece, length), jnp.float32),
        scratch_shapes=[pltpu.VMEM((piece, length), jnp.bfloat16)],
        compiler_params=pltpu.CompilerParams(vmem_limit_bytes=vmem_limit),
        cost_estimate=product_cost(piece, length, 1),
        name="final_transform",
    )(cosines, back)


def contract(left, right, left_dim, right_dim):
    return lax.dot_general(
        left, right, (((left_dim,), (right_dim,)), ((), ())), preferred_element_type=jnp.float32
    )


def neighbour_rows(slices):
    count = lax.axis_size("strip")
    head = slices[:, :margin]
    tail = slices[:, -margin:]
    above = lax.ppermute(tail, "strip", [(i, i + 1) for i in range(count - 1)])
    below = lax.ppermute(head, "strip", [(i + 1, i) for i in range(count - 1)])
    return above, below


def merged_rows_plain(slices, above, below):
    padded = jnp.concatenate([above, slices, below], axis=1).astype(jnp.float32)
    center = slices.astype(jnp.float32)
    count = center.shape[1]
    weight = floor_weight
    for d, share in zip(spacings, (1.0, 0.5, 0.25)):
        widened = jnp.pad(center, ((0, 0), (0, 0), (d, d)))
        term = padded[:, margin + d : margin + d + count] + padded[:, margin - d : margin - d + count]
        term = term + widened[:, :, 2 * d :] + widened[:, :, : -2 * d] - 4.0 * center
        weight = weight + share * term * term
    numerator = jnp.sum(weight * center, axis=0)
    denominator = jnp.sum(weight, axis=0)
    numerator = lax.psum_scatter(numerator, "focus", scatter_dimension=0, tiled=True)
    denominator = lax.psum_scatter(denominator, "focus", scatter_dimension=0, tiled=True)
    return (numerator / denominator).astype(jnp.bfloat16)


def merged_rows(slices, above, below, piece):
    focus = lax.axis_index("focus")
    rows = slices.shape[1]
    filler = jnp.zeros((slices.shape[0], edge - margin, slices.shape[2]), slices.dtype)
    above = jnp.concatenate([filler, above], axis=1)
    below = jnp.concatenate([below, filler], axis=1)
    inner_above = slices[:, piece - edge : piece]
    inner_below = slices[:, piece : piece + edge]

    def sums(half):
        top = jnp.where(half == 0, above, inner_above)
        bottom = jnp.where(half == 0, inner_below, below)
        return stencil(slices, half, top, bottom, piece)

    swap = [(0, 1), (1, 0)]
    for_partner = sums(1 - focus)
    arrived = [lax.ppermute(part, "focus", swap) for part in for_partner]
    own = sums(focus)
    return ((own[0] + arrived[0]) / (own[1] + arrived[1])).astype(jnp.bfloat16)


def body(slices, otf_rows, otf_cols):
    focus_count = lax.axis_size("focus")
    strip_count = lax.axis_size("strip")
    length = slices.shape[2]
    piece = length // (focus_count * strip_count)
    owners = ("focus", "strip")
    above, below = neighbour_rows(slices)
    owner = lax.axis_index("focus") * strip_count + lax.axis_index("strip")
    local_cols = lax.dynamic_slice_in_dim(otf_cols, owner * piece, piece, 0)
    if piece % lanes == 0 and focus_count == 2 and length % 512 == 0:
        cosines = cosine_table(length)
        block = max(512, piece)
        rows = merged_rows(slices, above, below, piece)
        along_cols = row_transform(cosines, rows, block)
        arrived = lax.all_to_all(along_cols, owners, split_axis=0, concat_axis=0, tiled=True)
        places = [s * focus_count + f for f in range(focus_count) for s in range(strip_count)]
        back = column_transform(cosines, arrived, otf_rows, local_cols, places, block)
        back = lax.all_to_all(back, owners, split_axis=0, concat_axis=0, tiled=True)
        return final_transform(cosines, back, block)
    cosines = cosine_table_plain(length)
    rows = merged_rows_plain(slices, above, below)
    along_cols = contract(cosines, rows, 1, 1).astype(jnp.bfloat16)
    arrived = lax.all_to_all(along_cols, owners, split_axis=0, concat_axis=1, tiled=True)
    column_block = (
        arrived.reshape(piece, focus_count, strip_count, piece)
        .transpose(0, 2, 1, 3)
        .reshape(piece, length)
    )
    spectrum = contract(column_block, cosines, 1, 1)
    response = local_cols[:, None] * otf_rows[None, :]
    filtered = (spectrum * (response / (response * response + noise_ratio))).astype(jnp.bfloat16)
    back_cols = contract(cosines, filtered, 0, 1).astype(jnp.bfloat16)
    rows_back = lax.all_to_all(back_cols, owners, split_axis=0, concat_axis=1, tiled=True)
    return jnp.dot(rows_back, cosines, preferred_element_type=jnp.float32)


def solution(mesh):
    in_specs = (P(("field", "focus"), "strip", None), P(), P())
    out_specs = P(("field", "focus", "strip"), None)
    return jax.shard_map(body, mesh=mesh, in_specs=in_specs, out_specs=out_specs, check_vma=False)
```

```python
import functools
import math

import jax
import jax.numpy as jnp
import numpy as np
from jax import lax
from jax.experimental import pallas as pl
from jax.experimental.pallas import tpu as pltpu
from jax.sharding import PartitionSpec as P

floor_weight = 0.01
noise_ratio = 0.01
spacings = (1, 2, 4)
margin = 4
edge = 16
lanes = 128
vmem_limit = 56 * 1024 * 1024


def band_matrices(height):
    band = np.zeros((3, height, height), np.float32)
    ends = np.zeros((3, 2, 8, 2 * edge), np.float32)
    for which, d in enumerate(spacings):
        band[which] = np.eye(height, k=d) + np.eye(height, k=-d) - 4.0 * np.eye(height)
        for r in range(d):
            ends[which, 0, r, edge + r - d] = 1.0
            ends[which, 1, 7 - r, edge + d - 1 - r] = 1.0
    return (
        jnp.asarray(band.reshape(3 * height, height), jnp.bfloat16),
        jnp.asarray(ends.reshape(48, 2 * edge), jnp.bfloat16),
    )


def table_kernel(high_cos, high_sin, low_cos, low_sin, out):
    value = high_cos[0] * low_cos[...] - high_sin[0] * low_sin[...]
    out[...] = value.astype(out.dtype)

    @pl.when(pl.program_id(0) == 0)
    def _():
        top = high_cos[0] * low_cos[:16, :] - high_sin[0] * low_sin[:16, :]
        row = lax.broadcasted_iota(jnp.int32, top.shape, 0)
        out[:16, :] = jnp.where(row == 0, top * math.sqrt(0.5), top).astype(out.dtype)


def cosine_table(length):
    low_count = 1 << (int(math.log2(length)) // 2)
    high_count = length // low_count
    sample = 2 * np.arange(length, dtype=np.int64) + 1
    unit = math.pi / (2 * length)
    high = (low_count * np.arange(high_count)[:, None] * sample) % (4 * length) * unit
    low = (np.arange(low_count)[:, None] * sample) % (4 * length) * unit
    scale = math.sqrt(2.0 / length)
    high_cos = jnp.asarray(scale * np.cos(high), jnp.float32)[:, None, :]
    high_sin = jnp.asarray(scale * np.sin(high), jnp.float32)[:, None, :]
    low_cos = jnp.asarray(np.cos(low), jnp.float32)
    low_sin = jnp.asarray(np.sin(low), jnp.float32)
    high_block = pl.BlockSpec((1, 1, length), lambda k: (k, 0, 0))
    low_block = pl.BlockSpec((low_count, length), lambda k: (0, 0))
    return pl.pallas_call(
        table_kernel,
        grid=(high_count,),
        in_specs=[high_block, high_block, low_block, low_block],
        out_specs=pl.BlockSpec((low_count, length), lambda k: (k, 0)),
        out_shape=jax.ShapeDtypeStruct((length, length), jnp.bfloat16),
        compiler_params=pltpu.CompilerParams(vmem_limit_bytes=vmem_limit),
        cost_estimate=pl.CostEstimate(
            flops=3 * length * length, bytes_accessed=2 * length * length, transcendentals=0
        ),
        name="cosine_table",
    )(high_cos, high_sin, low_cos, low_sin)


def cosine_block(first_row, height, length):
    low_count = min(64, length)
    high_count = length // low_count
    frequency = first_row + lax.broadcasted_iota(jnp.int32, (height, 1), 0)
    high_sample = lax.broadcasted_iota(jnp.int32, (1, high_count), 1)
    low_sample = lax.broadcasted_iota(jnp.int32, (1, low_count), 1)
    high_phase = 2 * low_count * high_sample * frequency % (4 * length)
    low_phase = (2 * low_sample + 1) * frequency % (4 * length)
    unit = jnp.float32(math.pi / (2 * length))
    high_angle = high_phase.astype(jnp.float32) * unit
    low_angle = low_phase.astype(jnp.float32) * unit
    norming = jnp.where(
        frequency == 0, jnp.float32(math.sqrt(1.0 / length)), jnp.float32(math.sqrt(2.0 / length))
    )
    high_cos = (norming * jnp.cos(high_angle))[:, :, None]
    high_sin = (norming * jnp.sin(high_angle))[:, :, None]
    low_cos = jnp.cos(low_angle)[:, None, :]
    low_sin = jnp.sin(low_angle)[:, None, :]
    table = high_cos * low_cos - high_sin * low_sin
    return table.reshape(height, length).astype(jnp.bfloat16)


def cosine_table_plain(length):
    height = min(512, length)
    starts = jnp.arange(length // height, dtype=jnp.int32) * height
    return lax.map(lambda first_row: cosine_block(first_row, height, length), starts).reshape(
        length, length
    )


def stencil_kernel(width, half, main, top, bottom, band, ends, num, den, terms_a, terms_b):
    del half
    height, length = main.shape[1], main.shape[2]
    chunks = length // width

    @pl.when(pl.program_id(0) == 0)
    def _():
        num[...] = jnp.zeros_like(num)
        den[...] = jnp.zeros_like(den)

    def vertical(chunk, terms):
        at = pl.ds(pl.multiple_of(chunk * width, width), width)
        terms[...] = jnp.dot(band[...], main[0, :, at], preferred_element_type=jnp.float32)
        outside = jnp.concatenate([top[0, :, at], bottom[0, :, at]], axis=0)
        extra = jnp.dot(ends[...], outside, preferred_element_type=jnp.float32)
        for which in range(3):
            base = which * height
            terms[base : base + 8, :] += extra[16 * which : 16 * which + 8]
            terms[base + height - 8 : base + height, :] += extra[16 * which + 8 : 16 * which + 16]

    def weigh(chunk, terms):
        start = chunk * width
        at = pl.ds(pl.multiple_of(start, width), width)
        before = pl.ds(pl.multiple_of(jnp.maximum(start - lanes, 0), lanes), lanes)
        after = pl.ds(pl.multiple_of(jnp.minimum(start + width, length - lanes), lanes), lanes)
        has_before = jnp.where(chunk > 0, 1.0, 0.0)
        has_after = jnp.where(chunk < chunks - 1, 1.0, 0.0)
        for row in range(0, height, 16):
            rows = slice(row, row + 16)
            center = main[0, rows, at].astype(jnp.float32)
            wide = jnp.concatenate(
                [
                    main[0, rows, before].astype(jnp.float32) * has_before,
                    center,
                    main[0, rows, after].astype(jnp.float32) * has_after,
                ],
                axis=1,
            )
            full = wide.shape[1]
            lap = []
            for which, d in enumerate(spacings):
                sides = pltpu.roll(wide, d, 1) + pltpu.roll(wide, full - d, 1)
                base = which * height + row
                lap.append(terms[base : base + 16, :] + sides[:, lanes : lanes + width])
            weight = (floor_weight + lap[0] * lap[0]) + 0.5 * (
                lap[1] * lap[1] + 0.5 * (lap[2] * lap[2])
            )
            num[rows, at] += weight * center
            den[rows, at] += weight

    vertical(0, terms_a)

    def pair(index, carry):
        chunk = 2 * index
        vertical(chunk + 1, terms_b)
        weigh(chunk, terms_a)
        vertical(jnp.minimum(chunk + 2, chunks - 1), terms_a)
        weigh(chunk + 1, terms_b)
        return carry

    lax.fori_loop(0, chunks // 2, pair, 0)


def stencil(slices, half, top, bottom, height):
    count, _, length = slices.shape
    width = 512
    band, ends = band_matrices(height)
    sums = jax.ShapeDtypeStruct((height, length), jnp.float32)
    whole = lambda s, h: (0, 0)
    return pl.pallas_call(
        functools.partial(stencil_kernel, width),
        grid_spec=pltpu.PrefetchScalarGridSpec(
            num_scalar_prefetch=1,
            grid=(count,),
            in_specs=[
                pl.BlockSpec((1, height, length), lambda s, h: (s, h[0], 0)),
                pl.BlockSpec((1, edge, length), lambda s, h: (s, 0, 0)),
                pl.BlockSpec((1, edge, length), lambda s, h: (s, 0, 0)),
                pl.BlockSpec(band.shape, whole),
                pl.BlockSpec(ends.shape, whole),
            ],
            out_specs=[pl.BlockSpec((height, length), whole)] * 2,
            scratch_shapes=[pltpu.VMEM((3 * height, width), jnp.float32)] * 2,
        ),
        out_shape=(sums, sums),
        compiler_params=pltpu.CompilerParams(vmem_limit_bytes=vmem_limit),
        cost_estimate=pl.CostEstimate(
            flops=count * height * length * 1600,
            bytes_accessed=count * height * length * 2 + height * length * 8,
            transcendentals=0,
        ),
        name="stencil",
    )(half.reshape(1), slices, top, bottom, band, ends)


def product_cost(rows, length, passes):
    return pl.CostEstimate(
        flops=2 * passes * rows * length * length,
        bytes_accessed=2 * length * length + 8 * rows * length,
        transcendentals=0,
    )


def row_kernel(table, rows, out):
    value = lax.dot_general(
        table[...], rows[...], (((1,), (1,)), ((), ())), preferred_element_type=jnp.float32
    )
    out[...] = value.astype(out.dtype).reshape(out.shape)


def row_transform(cosines, rows, block):
    piece, length = rows.shape
    return pl.pallas_call(
        row_kernel,
        grid=(length // block,),
        in_specs=[
            pl.BlockSpec((block, length), lambda k: (k, 0)),
            pl.BlockSpec((piece, length), lambda k: (0, 0)),
        ],
        out_specs=pl.BlockSpec((block // piece, piece, piece), lambda k: (k, 0, 0)),
        out_shape=jax.ShapeDtypeStruct((length // piece, piece, piece), jnp.bfloat16),
        compiler_params=pltpu.CompilerParams(vmem_limit_bytes=vmem_limit),
        cost_estimate=product_cost(piece, length, 1),
        name="row_transform",
    )(cosines, rows)


def column_kernel(places, table, arrived, rows_otf, cols_otf, out, columns, total):
    piece = arrived.shape[1]
    length = table.shape[1]
    step = pl.program_id(0)

    @pl.when(step == 0)
    def _():
        for source, place in enumerate(places):
            columns[:, place * piece : (place + 1) * piece] = arrived[source]

    spectrum = lax.dot_general(
        table[...], columns[...], (((1,), (1,)), ((), ())), preferred_element_type=jnp.float32
    )
    response = rows_otf[...] * cols_otf[...]
    filtered = spectrum * (response / (response * response + noise_ratio))
    turned = filtered.T.astype(jnp.bfloat16)
    part = 512
    for start in range(0, length, part):
        at = slice(start, start + part)
        value = jnp.dot(turned, table[:, at], preferred_element_type=jnp.float32)

        @pl.when(step == 0)
        def _():
            total[:, at] = value

        @pl.when(step > 0)
        def _():
            total[:, at] += value

    @pl.when(step == pl.num_programs(0) - 1)
    def _():
        for place in range(length // piece):
            out[place] = total[:, place * piece : (place + 1) * piece].astype(out.dtype)


def column_transform(cosines, arrived, rows_otf, cols_otf, places, block):
    count, piece, _ = arrived.shape
    length = count * piece
    whole = lambda u: (0, 0, 0)
    return pl.pallas_call(
        functools.partial(column_kernel, places),
        grid=(length // block,),
        in_specs=[
            pl.BlockSpec((block, length), lambda u: (u, 0)),
            pl.BlockSpec(arrived.shape, whole),
            pl.BlockSpec((block, 1), lambda u: (u, 0)),
            pl.BlockSpec((1, piece), lambda u: (0, 0)),
        ],
        out_specs=pl.BlockSpec((count, piece, piece), whole),
        out_shape=jax.ShapeDtypeStruct((count, piece, piece), jnp.bfloat16),
        scratch_shapes=[
            pltpu.VMEM((piece, length), jnp.bfloat16),
            pltpu.VMEM((piece, length), jnp.float32),
        ],
        compiler_params=pltpu.CompilerParams(vmem_limit_bytes=vmem_limit),
        cost_estimate=product_cost(piece, length, 2),
        name="column_transform",
    )(cosines, arrived, rows_otf[:, None], cols_otf[None, :])


def final_kernel(table, back, out, rows):
    @pl.when(pl.program_id(0) == 0)
    def _():
        count, piece, _ = back.shape
        for source in range(count):
            turned = back[source].astype(jnp.float32).T
            rows[:, source * piece : (source + 1) * piece] = turned.astype(jnp.bfloat16)

    out[...] = jnp.dot(rows[...], table[...], preferred_element_type=jnp.float32)


def final_transform(cosines, back, block):
    count, piece, _ = back.shape
    length = count * piece
    return pl.pallas_call(
        final_kernel,
        grid=(length // block,),
        in_specs=[
            pl.BlockSpec((length, block), lambda n: (0, n)),
            pl.BlockSpec(back.shape, lambda n: (0, 0, 0)),
        ],
        out_specs=pl.BlockSpec((piece, block), lambda n: (0, n)),
        out_shape=jax.ShapeDtypeStruct((piece, length), jnp.float32),
        scratch_shapes=[pltpu.VMEM((piece, length), jnp.bfloat16)],
        compiler_params=pltpu.CompilerParams(vmem_limit_bytes=vmem_limit),
        cost_estimate=product_cost(piece, length, 1),
        name="final_transform",
    )(cosines, back)


def contract(left, right, left_dim, right_dim):
    return lax.dot_general(
        left, right, (((left_dim,), (right_dim,)), ((), ())), preferred_element_type=jnp.float32
    )


def neighbour_rows(slices):
    count = lax.axis_size("strip")
    head = slices[:, :margin]
    tail = slices[:, -margin:]
    above = lax.ppermute(tail, "strip", [(i, i + 1) for i in range(count - 1)])
    below = lax.ppermute(head, "strip", [(i + 1, i) for i in range(count - 1)])
    return above, below


def merged_rows_plain(slices, above, below):
    padded = jnp.concatenate([above, slices, below], axis=1).astype(jnp.float32)
    center = slices.astype(jnp.float32)
    count = center.shape[1]
    weight = floor_weight
    for d, share in zip(spacings, (1.0, 0.5, 0.25)):
        widened = jnp.pad(center, ((0, 0), (0, 0), (d, d)))
        term = padded[:, margin + d : margin + d + count] + padded[:, margin - d : margin - d + count]
        term = term + widened[:, :, 2 * d :] + widened[:, :, : -2 * d] - 4.0 * center
        weight = weight + share * term * term
    numerator = jnp.sum(weight * center, axis=0)
    denominator = jnp.sum(weight, axis=0)
    numerator = lax.psum_scatter(numerator, "focus", scatter_dimension=0, tiled=True)
    denominator = lax.psum_scatter(denominator, "focus", scatter_dimension=0, tiled=True)
    return (numerator / denominator).astype(jnp.bfloat16)


def merged_rows(slices, above, below, piece):
    focus = lax.axis_index("focus")
    rows = slices.shape[1]
    filler = jnp.zeros((slices.shape[0], edge - margin, slices.shape[2]), slices.dtype)
    above = jnp.concatenate([filler, above], axis=1)
    below = jnp.concatenate([below, filler], axis=1)
    inner_above = slices[:, piece - edge : piece]
    inner_below = slices[:, piece : piece + edge]

    def sums(half):
        top = jnp.where(half == 0, above, inner_above)
        bottom = jnp.where(half == 0, inner_below, below)
        return stencil(slices, half, top, bottom, piece)

    swap = [(0, 1), (1, 0)]
    for_partner = sums(1 - focus)
    arrived = [lax.ppermute(part, "focus", swap) for part in for_partner]
    own = sums(focus)
    return ((own[0] + arrived[0]) / (own[1] + arrived[1])).astype(jnp.bfloat16)


def body(slices, otf_rows, otf_cols):
    focus_count = lax.axis_size("focus")
    strip_count = lax.axis_size("strip")
    length = slices.shape[2]
    piece = length // (focus_count * strip_count)
    owners = ("focus", "strip")
    above, below = neighbour_rows(slices)
    owner = lax.axis_index("focus") * strip_count + lax.axis_index("strip")
    local_cols = lax.dynamic_slice_in_dim(otf_cols, owner * piece, piece, 0)
    if piece % lanes == 0 and focus_count == 2 and length % 1024 == 0:
        cosines = cosine_table(length)
        block = max(512, piece)
        rows = merged_rows(slices, above, below, piece)
        along_cols = row_transform(cosines, rows, block)
        arrived = lax.all_to_all(along_cols, owners, split_axis=0, concat_axis=0, tiled=True)
        places = [s * focus_count + f for f in range(focus_count) for s in range(strip_count)]
        back = column_transform(cosines, arrived, otf_rows, local_cols, places, 2 * block)
        back = lax.all_to_all(back, owners, split_axis=0, concat_axis=0, tiled=True)
        return final_transform(cosines, back, block)
    cosines = cosine_table_plain(length)
    rows = merged_rows_plain(slices, above, below)
    along_cols = contract(cosines, rows, 1, 1).astype(jnp.bfloat16)
    arrived = lax.all_to_all(along_cols, owners, split_axis=0, concat_axis=1, tiled=True)
    column_block = (
        arrived.reshape(piece, focus_count, strip_count, piece)
        .transpose(0, 2, 1, 3)
        .reshape(piece, length)
    )
    spectrum = contract(column_block, cosines, 1, 1)
    response = local_cols[:, None] * otf_rows[None, :]
    filtered = (spectrum * (response / (response * response + noise_ratio))).astype(jnp.bfloat16)
    back_cols = contract(cosines, filtered, 0, 1).astype(jnp.bfloat16)
    rows_back = lax.all_to_all(back_cols, owners, split_axis=0, concat_axis=1, tiled=True)
    return jnp.dot(rows_back, cosines, preferred_element_type=jnp.float32)


def solution(mesh):
    in_specs = (P(("field", "focus"), "strip", None), P(), P())
    out_specs = P(("field", "focus", "strip"), None)
    return jax.shard_map(body, mesh=mesh, in_specs=in_specs, out_specs=out_specs, check_vma=False)
```
